32 devices in a mesh: groups: 2 (over x), mix: 16 (over z, y, core).
Axes of the slice: x: 2, y: 2, z: 4, core: 2. Of those that a mesh axis runs over, the one named last changes fastest.
Arguments:
- resid_in: bfloat16 [4096, 2048], P(('groups', 'mix')), parts along dimension 0, may hold values from -40 to 40
- head_in: bfloat16 [4096, 4096], P('groups', 'mix'), parts along dimension 0, may hold values from -6 to 6
- gate_in: bfloat16 [4096, 4096], P('groups', 'mix'), parts along dimension 0, may hold values from -64 to 64
- in_basis: bfloat16 [4096, 128], P('groups'), parts along dimension 0, may hold values from -6 to 6
- out_basis: bfloat16 [4096, 128], P('groups'), parts along dimension 0, may hold values from -6 to 6
- step_size: float32 [64, 4096], P('mix', 'groups'), parts along dimension 1, may hold values from 0 to 2
- decay_rate: float32 [64], P('mix'), may hold values from 0.5 to 2
- init_state: float32 [16, 64, 64, 128], P('groups', 'mix'), parts along dimension 0, may hold values from -0.6 to 0.6
- lengths: int32 [16], P('groups'), parts along dimension 0, may hold values from 1 to 512, 2048 in all
- norm_gain: float32 [4096], replicated, may hold values from 0.1 to 1.9
- out_proj: bfloat16 [4096, 2048], P('mix'), may hold values from -0.09375 to 0.09375
- moe_gain: float32 [2048], replicated, may hold values from 0.1 to 1.9
- expert_ids: int32 [4096, 8], P(('groups', 'mix')), parts along dimension 0, may hold values from 0 to 31, as said below
- route_weight: float32 [4096, 8], P(('groups', 'mix')), parts along dimension 0, may hold values from 0.1 to 0.4
- placement: int32 [32], replicated, may hold values from 0 to 31, each once
- w_gate: bfloat16 [32, 2048, 768], P('mix'), may hold values from -0.125 to 0.125
- w_up: bfloat16 [32, 2048, 768], P('mix'), may hold values from -0.125 to 0.125
- w_down: bfloat16 [32, 768, 2048], P('mix'), may hold values from -0.21875 to 0.21875
Outputs:
- layer_out: bfloat16 [4096, 2048], P(('groups', 'mix')), parts along dimension 0
The draws below stay inside these ranges and needn't reach their ends.
There are 2 independent parts, one for each index of `groups`. The reference program is written for one: setup_inputs(seed, part) draws one part's arguments, and reference() takes and returns one part's arrays. A program takes and returns all parts, laid end to end along the dimension named above; an argument that names none is the same for every part. Nothing has to cross between parts.
Inputs may be any that keep to these rules, and one draw needn't show every extreme that they name: `expert_ids`: each row names 8 different experts. Within each aligned block of 128 rows (one device's rows), 8 experts appear exactly 64 times each, 8 others 64 / 2 times each and the rest 64 / 4 times each; each of the three sets is the same in every block. `placement`: each slot once. `lengths`: requests fill the 2048 positions in order.
All inputs are finite; a program needn't handle non-finite values.
Results may differ from the reference program's by a relative error of at most 0.013.
Values may be sent and summed in bfloat16 or wider, within the bound.
A program may use at most 128 MiB of HBM per device.

```python
import math
import jax
import jax.numpy as jnp
import numpy as np
from jax import lax

D = 2048
HEADS = 64
HEAD_DIM = 64
STATE = 128
SPAN = 256
FFE = 768
TOPK = 8
REQUEST_COUNT = 8
TOK_DEV = 128
TOKEN_COUNT = 2048
EXPERTS = 32
MOST = 512
CAP = 64
N_MIX = 16


def draw_step_size(key, part):
    split_random_keys = jax.random.split(jax.random.fold_in(key, 11), 6)
    fast_heads = jax.random.uniform(split_random_keys[0], (HEADS,)) < 0.5
    fast_base = jax.random.uniform(split_random_keys[1], (HEADS,), minval=0.03, maxval=0.06)
    slow_base = jax.random.uniform(split_random_keys[2], (HEADS,), minval=0.1, maxval=0.3) / MOST
    baseline_rate = jnp.where(fast_heads, fast_base, slow_base)
    random_offset = jnp.exp(jax.random.uniform(split_random_keys[3], (HEADS, TOKEN_COUNT), minval=math.log(0.5), maxval=math.log(2.0)))
    spike_position = jax.random.randint(split_random_keys[4], (2 * REQUEST_COUNT,), 0, TOKEN_COUNT)
    spike_length = jax.random.uniform(split_random_keys[5], (2 * REQUEST_COUNT,), minval=0.25, maxval=0.5)
    spike_events = jnp.zeros((TOKEN_COUNT,), jnp.float32).at[spike_position].set(spike_length)
    return (baseline_rate[:, None] * random_offset + spike_events[None, :]).astype(jnp.float32)


def draw_gate_in(key, part):
    split_random_keys = jax.random.split(jax.random.fold_in(key, 23), 3)
    width_all = HEADS * HEAD_DIM
    head_share = (jnp.arange(width_all) // HEAD_DIM).astype(jnp.float32) / (HEADS - 1)
    row_scale = jnp.exp(jax.random.uniform(split_random_keys[0], (TOKEN_COUNT, 1), minval=math.log(0.3), maxval=math.log(3.0)))
    col_scale = jnp.exp(jax.random.uniform(split_random_keys[1], (1, width_all), minval=math.log(0.3), maxval=math.log(3.0)))
    trend = 3.0 ** (0.5 * head_share)
    noise = jax.random.truncated_normal(split_random_keys[2], -4.0, 4.0, (TOKEN_COUNT, width_all))
    return (noise * row_scale * col_scale * trend[None, :]).astype(jnp.bfloat16)


def draw_resid_in(key, part):
    split_random_keys = jax.random.split(jax.random.fold_in(key, 37), 3)
    row_scale = jnp.exp(jax.random.uniform(split_random_keys[0], (TOKEN_COUNT, 1), minval=math.log(0.3), maxval=math.log(3.0)))
    col_scale = jnp.exp(jax.random.uniform(split_random_keys[1], (1, D), minval=math.log(0.3), maxval=math.log(3.0)))
    noise = jax.random.truncated_normal(split_random_keys[2], -4.0, 4.0, (TOKEN_COUNT, D))
    return (noise * row_scale * col_scale).astype(jnp.bfloat16)


def draw_expert_ids(key, part):
    blocks_count = TOKEN_COUNT // TOK_DEV
    order_key, block_key = jax.random.split(jax.random.fold_in(key, 41))
    ranking = jax.random.permutation(order_key, jnp.arange(EXPERTS, dtype=jnp.int32))
    position = jnp.arange(EXPERTS, dtype=jnp.int32)
    level = jnp.where(position < EXPERTS // 4, 0, jnp.where(position < EXPERTS // 2, 1, 2)).astype(jnp.int32)
    per_level = jnp.where(level == 0, CAP, jnp.where(level == 1, CAP // 2, CAP // 4)).astype(jnp.int32)

    def one_block(block_seed):
        first_key, second_key, third_key = jax.random.split(block_seed, 3)
        jitter_rank = jax.random.randint(first_key, (EXPERTS,), 0, EXPERTS).astype(jnp.int32)
        score_value = (level * EXPERTS + jitter_rank) * EXPERTS + position
        within = jnp.argsort(score_value, stable=True)
        shuffled = ranking[within]
        mixing = jax.random.permutation(second_key, jnp.arange(EXPERTS, dtype=jnp.int32))
        labels = jnp.repeat(shuffled[mixing], per_level[mixing], total_repeat_length=TOK_DEV * TOPK)
        table = labels.reshape(TOPK, TOK_DEV).T
        row_order = jax.random.permutation(third_key, jnp.arange(TOK_DEV, dtype=jnp.int32))
        return table[row_order]
    block_seeds = jax.random.split(block_key, blocks_count)
    return jax.vmap(one_block)(block_seeds).reshape(TOKEN_COUNT, TOPK).astype(jnp.int32)


def levels(rng, extent, shards, smallest, high):
    def one(dim, shards_of):
        draws = jax.random.uniform(jax.random.fold_in(jax.random.fold_in(rng, 6), dim), (shards_of,), jnp.float32, smallest / len(shards), high / len(shards))
        return jnp.repeat(jnp.exp(draws), extent[dim] // shards_of).reshape((-1,) + (1,) * (len(extent) - dim - 1))

    gain = one(*shards[0])
    for cut in shards[1:]:
        gain = gain * one(*cut)
    return gain


def split_up(number_of, total, most, skew):
    portions = [(1 << 20) // math.isqrt(standing ** skew) + 1 for standing in range(2, number_of + 1)]
    rest, given = total - most - (number_of - 1), [1] * (number_of - 1)
    while rest > 0:
        candidates = [i for i in range(number_of - 1) if given[i] < most]
        mass, budget = sum([portions[i] for i in candidates]), rest
        for i in candidates:
            extra = min(most - given[i], max(1, budget * portions[i] // mass), rest)
            given[i] = given[i] + extra
            rest = rest - extra
    return np.array([most] + given)


def ragged(own_key, amount, total, bound, skew):
    if amount == 2:
        one = jax.random.randint(own_key, (), max(1, total - bound), min(bound, total - 1) + 1)
        return jnp.stack([one, total - one])
    sizes = jnp.asarray(split_up(amount, total, bound, skew), jnp.int32)
    couples = (amount - 1) // 2
    giver, sink = sizes[1:1 + 2 * couples:2], sizes[2:2 + 2 * couples:2]
    room = jnp.minimum(giver - 1, bound - sink)
    passed = jax.random.randint(jax.random.fold_in(own_key, 1), (couples,), 0, 1 << 20) % (room + 1)
    sizes = sizes.at[1:1 + 2 * couples:2].set(giver - passed).at[2:2 + 2 * couples:2].set(sink + passed)
    return sizes[jax.random.permutation(jax.random.fold_in(own_key, 2), amount)]


def bell_draw(key, dims, scale, bound, shards=(), held_as=jnp.bfloat16):
    drawn = scale * jax.random.normal(key, dims, jnp.float32)
    if shards:
        drawn = drawn * levels(key, dims, shards, -0.22, 0.18)
    return jnp.clip(drawn, -bound, bound).astype(held_as)


def setup_inputs(seed: int = 0, part: int = 0) -> dict:
    seeds = jax.random.split(jax.random.key(seed), 19)
    own_keys = jax.random.split(jax.random.fold_in(seeds[18], part), 19)
    return {
        "resid_in": draw_resid_in(jax.random.fold_in(jax.random.fold_in(seeds[18], part), 71), part),
        "head_in": bell_draw(own_keys[1], (TOKEN_COUNT, HEADS * HEAD_DIM), 1.0, 6.0, ((1, 16),)),
        "gate_in": draw_gate_in(jax.random.fold_in(jax.random.fold_in(seeds[18], part), 71), part),
        "in_basis": bell_draw(own_keys[3], (TOKEN_COUNT, STATE), 1.0, 6.0),
        "out_basis": bell_draw(own_keys[4], (TOKEN_COUNT, STATE), 1.0, 6.0),
        "step_size": draw_step_size(jax.random.fold_in(jax.random.fold_in(seeds[18], part), 71), part),
        "decay_rate": jnp.clip(jnp.exp(math.log(2.0) - 1.3862944 * jax.random.uniform(seeds[6], (HEADS,), jnp.float32) ** levels(seeds[6], (HEADS,), ((0, 16),), -0.2, 0.2)), 0.5, 2.0),
        "init_state": bell_draw(own_keys[7], (REQUEST_COUNT, HEADS, HEAD_DIM, STATE), 0.1, 0.6, ((1, 16),), jnp.float32),
        "lengths": ragged(own_keys[8], REQUEST_COUNT, TOKEN_COUNT, MOST, 2).astype(jnp.int32),
        "norm_gain": jnp.clip(1.0 + 0.18 * jax.random.normal(seeds[9], (HEADS * HEAD_DIM,), jnp.float32), 0.1, 1.9),
        "out_proj": bell_draw(seeds[10], (HEADS * HEAD_DIM, D), (HEADS * HEAD_DIM) ** -0.5, 0.09375, ((0, 16),)),
        "moe_gain": jnp.clip(1.0 + 0.18 * jax.random.normal(seeds[11], (D,), jnp.float32), 0.1, 1.9),
        "expert_ids": draw_expert_ids(jax.random.fold_in(jax.random.fold_in(seeds[18], part), 71), part),
        "route_weight": jnp.clip(0.1 + 0.3 * jax.random.uniform(own_keys[13], (TOKEN_COUNT, TOPK), jnp.float32) ** levels(own_keys[13], (TOKEN_COUNT, TOPK), ((0, 16),), -0.2, 0.2), 0.1, 0.4),
        "placement": jax.random.permutation(seeds[14], EXPERTS).astype(jnp.int32),
        "w_gate": bell_draw(seeds[15], (EXPERTS, D, FFE), D ** -0.5, 0.125, ((0, 16),)),
        "w_up": bell_draw(seeds[16], (EXPERTS, D, FFE), D ** -0.5, 0.125, ((0, 16),)),
        "w_down": bell_draw(seeds[17], (EXPERTS, FFE, D), FFE ** -0.5, 0.21875, ((0, 16),)),
    }


epsilon = 1e-05

def request_layout(lengths, tokens_total):
    request_end = jnp.cumsum(lengths).astype(jnp.int32)
    request_first = (request_end - lengths).astype(jnp.int32)
    position = jnp.arange(tokens_total, dtype=jnp.int32)
    segment = lax.optimization_barrier(jnp.sum((position[None, :] >= request_end[:, None]).astype(jnp.int32), axis=0)).astype(jnp.int32)
    member = segment[None, :] == jnp.arange(lengths.shape[0], dtype=jnp.int32)[:, None]
    first_of = lax.optimization_barrier(jnp.sum(jnp.where(member, request_first[:, None], 0), axis=0)).astype(jnp.int32)
    return (segment, first_of, member)

def scan_head(head_values, head_steps, head_rate, in_basis, out_basis, state_init, segment, first_of, member, block_len):
    tokens_total = head_values.shape[0]
    blocks = tokens_total // block_len
    highest = lax.Precision.HIGHEST
    log_decay = -head_steps * head_rate
    driven = head_values.astype(jnp.float32) * head_steps[:, None]

    def split_rows(array):
        return array.reshape((blocks, block_len) + array.shape[1:])
    block_first = jnp.arange(blocks, dtype=jnp.int32) * block_len
    member_blocks = member.reshape(member.shape[0], blocks, block_len).transpose(1, 0, 2)
    inputs = (split_rows(driven), split_rows(log_decay), split_rows(in_basis), split_rows(out_basis), split_rows(segment), split_rows(first_of), member_blocks, block_first)
    offsets = jnp.arange(block_len, dtype=jnp.int32)
    causal = offsets[None, :] <= offsets[:, None]

    def advance(state_in, block_in):
        drive_block, decay_block, basis_block, readout_block, segment_block, first_block, member_block, first_pos = block_in
        basis_wide = basis_block.astype(jnp.float32)
        readout_wide = readout_block.astype(jnp.float32)
        running = jnp.cumsum(decay_block)
        earlier = running - decay_block
        same_seq = (segment_block[:, None] == segment_block[None, :]) & causal
        gap_values = jnp.minimum(running[:, None] - running[None, :], 0.0)
        kernel = jnp.where(same_seq, jnp.exp(gap_values), 0.0)
        scores = jnp.dot(readout_block, basis_block.T, preferred_element_type=jnp.float32)
        output = jnp.dot(kernel * scores, drive_block, precision=highest)
        before = lax.optimization_barrier(jnp.max(jnp.where(same_seq, earlier[None, :], -jnp.inf), axis=1))
        carried = first_block < first_pos
        weight = jnp.exp(running - before)
        from_state = jnp.dot(readout_wide, state_in.T, precision=highest)
        projected = jnp.einsum('qn,rpn->rqp', readout_wide, state_init, precision=highest)
        from_init = lax.optimization_barrier(jnp.sum(member_block.astype(jnp.float32)[:, :, None] * projected, axis=0))
        output = output + weight[:, None] * jnp.where(carried[:, None], from_state, from_init)
        last_weight = jnp.where(same_seq[-1], jnp.exp(running[-1] - running), 0.0)
        state_out = jnp.dot((drive_block * last_weight[:, None]).T, basis_wide, precision=highest)
        init_last = jnp.einsum('r,rpn->pn', member_block[:, -1].astype(jnp.float32), state_init, precision=highest)
        source = jnp.where(carried[-1], state_in, init_last)
        state_out = state_out + weight[-1] * source
        return (state_out, output)
    empty_state = jnp.zeros((head_values.shape[1], in_basis.shape[1]), jnp.float32)
    _, outputs = lax.scan(advance, empty_state, inputs)
    return outputs.reshape(tokens_total, -1)

def reference(resid_in, head_in, gate_in, in_basis, out_basis, step_size, decay_rate, init_state, lengths, norm_gain, out_proj, moe_gain, expert_ids, route_weight, placement, w_gate, w_up, w_down):
    segment, first_of, member = request_layout(lengths, TOKEN_COUNT)
    head_inputs = head_in.reshape(TOKEN_COUNT, HEADS, HEAD_DIM).transpose(1, 0, 2)
    head_states = init_state.transpose(1, 0, 2, 3)

    def one_head(packed):
        head_values, head_steps, head_rate, state_init = packed
        return scan_head(head_values, head_steps, head_rate, in_basis, out_basis, state_init, segment, first_of, member, SPAN)
    head_outputs = lax.map(one_head, (head_inputs, step_size, decay_rate, head_states))
    scan_out = head_outputs.transpose(1, 0, 2).reshape(TOKEN_COUNT, HEADS * HEAD_DIM)
    gated_out = scan_out * jax.nn.silu(gate_in.astype(jnp.float32))
    squares = lax.optimization_barrier(jnp.sum(gated_out * gated_out, axis=1))
    mixed_in = (gated_out * norm_gain).astype(jnp.bfloat16)
    group_inputs = mixed_in.reshape(TOKEN_COUNT, N_MIX, -1).transpose(1, 0, 2)
    group_weights = out_proj.reshape(N_MIX, -1, D)

    def add_group(running_sum, packed):
        group_in, group_weight = packed
        group_term = jnp.dot(group_in, group_weight, preferred_element_type=jnp.float32).astype(jnp.bfloat16)
        group_term = lax.optimization_barrier(group_term)
        return (running_sum + group_term.astype(jnp.float32), None)
    mixer_sum, _ = lax.scan(add_group, jnp.zeros((TOKEN_COUNT, D), jnp.float32), (group_inputs, group_weights))
    mixer_out = mixer_sum * lax.rsqrt(squares / (HEADS * HEAD_DIM) + epsilon)[:, None]
    hidden = resid_in.astype(jnp.float32) + mixer_out
    normed = (hidden * lax.rsqrt(lax.optimization_barrier(jnp.mean(hidden * hidden, axis=1, keepdims=True)) + epsilon) * moe_gain).astype(jnp.bfloat16)
    flat_ids = expert_ids.reshape(-1).astype(jnp.int32)
    choose = (flat_ids[:, None] == jnp.arange(EXPERTS, dtype=jnp.int32)[None, :]).astype(jnp.int32)
    slot_rank = (lax.optimization_barrier(jnp.sum(jnp.cumsum(choose, axis=0) * choose, axis=1)) - 1).astype(jnp.int32)
    capacity = N_MIX * CAP
    token_of_pair = (jnp.arange(TOKEN_COUNT * TOPK, dtype=jnp.int32) // TOPK).astype(jnp.int32)
    token_table = jnp.zeros((EXPERTS, capacity), jnp.int32).at[flat_ids, slot_rank].set(token_of_pair)
    weight_table = jnp.zeros((EXPERTS, capacity), jnp.float32).at[flat_ids, slot_rank].set(route_weight.reshape(-1))

    def add_expert(expert_sum, expert):
        slot_index = placement[expert]
        picked_tokens = token_table[expert]
        chosen = jnp.take(normed, picked_tokens, axis=0)
        gate_part = jnp.dot(chosen, w_gate[slot_index], preferred_element_type=jnp.float32)
        up_part = jnp.dot(chosen, w_up[slot_index], preferred_element_type=jnp.float32)
        inner_act = (jax.nn.silu(gate_part) * up_part).astype(jnp.bfloat16)
        result = jnp.dot(inner_act, w_down[slot_index], preferred_element_type=jnp.float32).astype(jnp.bfloat16)
        result = lax.optimization_barrier(result)
        expert_sum = expert_sum.at[picked_tokens].add(weight_table[expert][:, None] * result.astype(jnp.float32))
        return (expert_sum, None)
    expert_sum, _ = lax.scan(add_expert, jnp.zeros((TOKEN_COUNT, D), jnp.float32), jnp.arange(EXPERTS, dtype=jnp.int32))
    return (hidden + expert_sum).astype(jnp.bfloat16)
```

```python
import functools

import jax
import jax.numpy as jnp
from jax import lax
from jax.experimental import pallas as pl
from jax.experimental.pallas import tpu as pltpu
from jax.sharding import PartitionSpec as P

HEADS = 64
HEAD_DIM = 64
SPAN = 256
MESH = pl.DeviceIdType.MESH
NT = (((1,), (1,)), ((), ()))
TN = (((0,), (0,)), ((), ()))

epsilon = 1e-05


def scan_kernel(
    requests,
    heads,
    width,
    first_ref,
    x_ref,
    gate_ref,
    basis_ref,
    readout_ref,
    step_ref,
    decay_ref,
    init_ref,
    gain_ref,
    mixed_ref,
    square_ref,
    state_ref,
    source_ref,
):
    block = pl.program_id(0)
    rows = x_ref.shape[0]
    lanes = heads * width
    start = block * rows
    highest = lax.Precision.HIGHEST

    @pl.when(block == 0)
    def _():
        state_ref[...] = jnp.zeros_like(state_ref)

    pos_col = start + lax.broadcasted_iota(jnp.int32, (rows, 1), 0)
    pos_row = start + lax.broadcasted_iota(jnp.int32, (1, rows), 1)
    seg_col = jnp.zeros((rows, 1), jnp.int32)
    seg_row = jnp.zeros((1, rows), jnp.int32)
    seg_first = jnp.int32(0)
    seg_last = jnp.int32(0)
    for r in range(1, requests):
        first = first_ref[r]
        seg_col += (pos_col >= first).astype(jnp.int32)
        seg_row += (pos_row >= first).astype(jnp.int32)
        seg_first += (start >= first).astype(jnp.int32)
        seg_last += (start + rows - 1 >= first).astype(jnp.int32)
    carries = first_ref[seg_first] < start
    carries_last = first_ref[seg_last] < start
    same = (seg_col == seg_row) & (pos_row <= pos_col)
    total_col = lax.dot_general(
        same.astype(jnp.float32),
        decay_ref[...],
        NT,
        precision=highest,
        preferred_element_type=jnp.float32,
    )
    total_row = total_col.T
    step_row = step_ref[...]
    step_col = step_row.T
    readout = readout_ref[...]
    basis = basis_ref[...]
    scores = lax.dot_general(readout, basis, NT, preferred_element_type=jnp.float32)
    scores = jnp.where(same, scores, 0.0)

    def read(state):
        high = state.astype(jnp.bfloat16)
        low = (state - high.astype(jnp.float32)).astype(jnp.bfloat16)
        return lax.dot_general(
            readout, high, NT, preferred_element_type=jnp.float32
        ) + lax.dot_general(readout, low, NT, preferred_element_type=jnp.float32)

    carried = (seg_col == seg_first) & carries
    source_ref[...] = jnp.where(carried, read(state_ref[...]), 0.0)
    for r in range(requests):
        first = first_ref[r]

        @pl.when((first >= start) & (first < start + rows))
        def _(r=r):
            source_ref[...] += jnp.where(seg_col == r, read(init_ref[r]), 0.0)

    lane = lax.broadcasted_iota(jnp.int32, (1, lanes), 1)

    def spread(columns):
        out = columns[:, 0:1]
        for h in range(1, heads):
            out = jnp.where(lane >= h * width, columns[:, h : h + 1], out)
        return jnp.broadcast_to(out, (columns.shape[0], lanes))

    x = x_ref[...]
    parts = []
    for h in range(heads):
        gap = jnp.minimum(total_col[:, h : h + 1] - total_row[h : h + 1, :], 0.0)
        weight = jnp.exp(gap) * scores * step_row[h : h + 1, :]
        parts.append(
            jnp.dot(
                weight.astype(jnp.bfloat16),
                x[:, h * width : (h + 1) * width],
                preferred_element_type=jnp.float32,
            )
        )
    out = jnp.concatenate(parts, axis=1)
    out = out + spread(jnp.exp(total_col)) * source_ref[...]

    gate = gate_ref[...].astype(jnp.float32)
    gated = out * (gate / (1.0 + jnp.exp(-gate)))
    square_ref[...] = lax.dot_general(
        jnp.ones((8, lanes), jnp.float32),
        gated * gated,
        NT,
        precision=highest,
        preferred_element_type=jnp.float32,
    )
    mixed_ref[...] = (gated * gain_ref[...]).astype(jnp.bfloat16)

    last = total_col[rows - 1 : rows, :]
    keep = jnp.where(
        seg_col == seg_last, jnp.exp(jnp.minimum(last - total_col, 0.0)), 0.0
    )
    drive = (x.astype(jnp.float32) * spread(keep * step_col)).astype(jnp.bfloat16)
    added = lax.dot_general(drive, basis, TN, preferred_element_type=jnp.float32)
    fade = jnp.exp(last)
    for h in range(heads):
        at = slice(h * width, (h + 1) * width)
        source = jnp.where(carries_last, state_ref[at, :], init_ref[seg_last, at, :])
        state_ref[at, :] = added[at, :] + fade[:, h : h + 1] * source


def scan(head_in, gate_in, in_basis, out_basis, step_size, decay_rate, init_state, lengths, gain):
    tokens, lanes = head_in.shape
    heads = step_size.shape[0]
    width = lanes // heads
    requests = lengths.shape[0]
    states = in_basis.shape[1]
    rows = SPAN
    order = jnp.arange(requests, dtype=jnp.int32)
    first = jnp.sum(jnp.where(order[None, :] < order[:, None], lengths[None, :], 0), axis=1)
    extra = (-heads) % 8
    step = jnp.pad(step_size, ((0, extra), (0, 0)))
    decay = jnp.pad(-step_size * decay_rate[:, None], ((0, extra), (0, 0)))
    padded = heads + extra
    init = init_state.reshape(requests, lanes, states)
    return pl.pallas_call(
        functools.partial(scan_kernel, requests, heads, width),
        grid=(tokens // rows,),
        in_specs=[
            pl.BlockSpec(memory_space=pltpu.SMEM),
            pl.BlockSpec((rows, lanes), lambda b: (b, 0)),
            pl.BlockSpec((rows, lanes), lambda b: (b, 0)),
            pl.BlockSpec((rows, states), lambda b: (b, 0)),
            pl.BlockSpec((rows, states), lambda b: (b, 0)),
            pl.BlockSpec((padded, rows), lambda b: (0, b)),
            pl.BlockSpec((padded, rows), lambda b: (0, b)),
            pl.BlockSpec((requests, lanes, states), lambda b: (0, 0, 0)),
            pl.BlockSpec((1, lanes), lambda b: (0, 0)),
        ],
        out_specs=[
            pl.BlockSpec((rows, lanes), lambda b: (b, 0)),
            pl.BlockSpec((8, rows), lambda b: (0, b)),
        ],
        out_shape=[
            jax.ShapeDtypeStruct((tokens, lanes), jnp.bfloat16),
            jax.ShapeDtypeStruct((8, tokens), jnp.float32),
        ],
        scratch_shapes=[
            pltpu.VMEM((lanes, states), jnp.float32),
            pltpu.VMEM((rows, lanes), jnp.float32),
        ],
        compiler_params=pltpu.CompilerParams(vmem_limit_bytes=40 * 2**20),
        name="scan",
    )(first, head_in, gate_in, in_basis, out_basis, step, decay, init, gain)


def ring_of(ring):
    me = lax.axis_index("mix")
    core = me % 2
    pair = me // 2
    side = pair % 2
    along = pair // 2
    place = (1 - side) * along + side * (ring - 1 - along)
    return me, core, place, 1 - 2 * core


def device_at(place, core, ring):
    far = place // (ring // 2)
    along = (1 - far) * place + far * (ring - 1 - place)
    return (2 * along + far) * 2 + core


def greet(devices):
    barrier = pltpu.get_barrier_semaphore()
    for device in devices:
        pl.semaphore_signal(barrier, inc=1, device_id={"mix": device}, device_id_type=MESH)
    pl.semaphore_wait(barrier, len(devices))


def remote(src, dst, send, recv, device):
    return pltpu.make_async_remote_copy(
        src_ref=src,
        dst_ref=dst,
        send_sem=send,
        recv_sem=recv,
        device_id={"mix": device},
        device_id_type=MESH,
    )


def gather_kernel(ring, cuts, x_ref, out_ref, local_sem, ring_send, ring_recv, pair_send, pair_recv):
    me, core, place, way = ring_of(ring)
    rows = x_ref.shape[0]
    piece = rows // cuts
    onward = device_at((place + way + ring) % ring, core, ring)
    behind = device_at((place - way + ring) % ring, core, ring)
    twin = 2 * (me // 2) + 1 - core
    greet([onward, behind, twin])
    own = pltpu.make_async_copy(x_ref, out_ref.at[pl.ds(me * rows, rows), :], local_sem)
    own.start()
    ring_copies = {}
    pair_copies = {}
    for step in range(ring):
        holder = device_at((place - step * way + 2 * ring) % ring, core, ring)
        for c in range(cuts):
            at = out_ref.at[pl.ds(holder * rows + c * piece, piece), :]
            if step > 0:
                ring_copies[step - 1, c].wait_recv()
            src = x_ref.at[pl.ds(c * piece, piece), :] if step == 0 else at
            if step < ring - 1:
                copy = remote(src, at, ring_send.at[step, c], ring_recv.at[step, c], onward)
                copy.start()
                ring_copies[step, c] = copy
            copy = remote(src, at, pair_send.at[step, c], pair_recv.at[step, c], twin)
            copy.start()
            pair_copies[step, c] = copy
    own.wait()
    for copy in ring_copies.values():
        copy.wait_send()
    for copy in pair_copies.values():
        copy.wait_send()
        copy.wait_recv()


def gather_rows(x, devices, collective_id):
    rows, columns = x.shape
    ring = devices // 2
    cuts = 2
    return pl.pallas_call(
        functools.partial(gather_kernel, ring, cuts),
        in_specs=[pl.BlockSpec(memory_space=pltpu.VMEM)],
        out_specs=pl.BlockSpec(memory_space=pl.ANY),
        out_shape=jax.ShapeDtypeStruct((devices * rows, columns), x.dtype),
        scratch_shapes=[
            pltpu.SemaphoreType.DMA,
            pltpu.SemaphoreType.DMA((ring, cuts)),
            pltpu.SemaphoreType.DMA((ring, cuts)),
            pltpu.SemaphoreType.DMA((ring, cuts)),
            pltpu.SemaphoreType.DMA((ring, cuts)),
        ],
        compiler_params=pltpu.CompilerParams(
            collective_id=collective_id, has_side_effects=True, vmem_limit_bytes=48 * 2**20
        ),
        name="gather_rows",
    )(x)


def reduce_kernel(
    ring,
    cuts,
    product,
    *refs,
):
    if product:
        mixed_ref, proj_ref, out_ref = refs[:3]
        refs = refs[3:]
        to_twin, mine, from_twin, sent, got = refs[:5]
        refs = refs[5:]
    else:
        terms_ref, out_ref = refs[:2]
        refs = refs[2:]
        mine, from_twin, sent, got = refs[:4]
        mine_sem = refs[-1]
        refs = refs[4:]
    pair_send, pair_recv, ring_send, ring_recv = refs[:4]
    me, core, place, way = ring_of(ring)
    rows = out_ref.shape[0]
    piece = rows // cuts
    onward = device_at((place + way + ring) % ring, core, ring)
    behind = device_at((place - way + ring) % ring, core, ring)
    twin = 2 * (me // 2) + 1 - core
    greet([onward, behind, twin])
    pair_copies = []
    mine_copies = []

    def give(step):
        theirs = device_at((place + (1 + step) * way) % ring, 1 - core, ring)
        if product:
            to_twin[step] = jnp.dot(
                mixed_ref[pl.ds(theirs * rows, rows), :],
                proj_ref[...],
                preferred_element_type=jnp.float32,
            ).astype(jnp.bfloat16)
            src = to_twin.at[step]
        else:
            src = terms_ref.at[pl.ds(theirs * rows, rows), :]
        copy = remote(src, from_twin.at[step], pair_send.at[step], pair_recv.at[step], twin)
        copy.start()
        pair_copies.append(copy)
        ours = device_at((place - (1 + step) * way + 2 * ring) % ring, core, ring)
        if product:
            mine[step] = jnp.dot(
                mixed_ref[pl.ds(ours * rows, rows), :],
                proj_ref[...],
                preferred_element_type=jnp.float32,
            ).astype(jnp.bfloat16)
        else:
            copy = pltpu.make_async_copy(
                terms_ref.at[pl.ds(ours * rows, rows), :], mine.at[step], mine_sem.at[step]
            )
            copy.start()
            mine_copies.append(copy)

    if product:
        give(0)
    else:
        for step in range(ring):
            give(step)
    ring_copies = {}
    for step in range(ring):
        if product and step + 1 < ring:
            give(step + 1)
        if not product:
            mine_copies[step].wait()
        pair_copies[step].wait_recv()
        for c in range(cuts):
            at = pl.ds(c * piece, piece)
            total = mine[step, at, :].astype(jnp.float32) + from_twin[step, at, :].astype(
                jnp.float32
            )
            if step > 0:
                ring_copies[step - 1, c].wait_recv()
                total = total + got[step - 1, at, :].astype(jnp.float32)
            if step < ring - 1:
                sent[step, at, :] = total.astype(jnp.bfloat16)
                copy = remote(
                    sent.at[step, at, :],
                    got.at[step, at, :],
                    ring_send.at[step, c],
                    ring_recv.at[step, c],
                    onward,
                )
                copy.start()
                ring_copies[step, c] = copy
            else:
                out_ref[at, :] = total
    for copy in pair_copies:
        copy.wait_send()
    for copy in ring_copies.values():
        copy.wait_send()


def reduce_rows(operands, rows, columns, devices, collective_id):
    product = len(operands) == 2
    ring = devices // 2
    cuts = 2
    block = pltpu.VMEM((ring, rows, columns), jnp.bfloat16)
    short = pltpu.VMEM((ring - 1, rows, columns), jnp.bfloat16)
    return pl.pallas_call(
        functools.partial(reduce_kernel, ring, cuts, product),
        in_specs=[pl.BlockSpec(memory_space=pltpu.VMEM if product else pl.ANY)] * len(operands),
        out_specs=pl.BlockSpec(memory_space=pltpu.VMEM),
        out_shape=jax.ShapeDtypeStruct((rows, columns), jnp.float32),
        scratch_shapes=([block] if product else [])
        + [block, block, short, short]
        + [
            pltpu.SemaphoreType.DMA((ring,)),
            pltpu.SemaphoreType.DMA((ring,)),
            pltpu.SemaphoreType.DMA((ring, cuts)),
            pltpu.SemaphoreType.DMA((ring, cuts)),
        ]
        + ([] if product else [pltpu.SemaphoreType.DMA((ring,))]),
        compiler_params=pltpu.CompilerParams(
            collective_id=collective_id, has_side_effects=True, vmem_limit_bytes=52 * 2**20
        ),
        name="reduce_products" if product else "reduce_rows",
    )(*operands)


def expert_kernel(
    experts, blocks, cap, x_ref, rank_ref, rank_row_ref, weight_ref, gate_hbm, up_hbm, down_hbm,
    out_ref, gate_ref, up_ref, down_ref, sems,
):
    first = pl.program_id(0) == 0
    rows = x_ref.shape[0] // blocks

    def copies(e):
        return [
            pltpu.make_async_copy(gate_hbm.at[e], gate_ref.at[e], sems.at[e, 0]),
            pltpu.make_async_copy(up_hbm.at[e], up_ref.at[e], sems.at[e, 1]),
            pltpu.make_async_copy(down_hbm.at[e], down_ref.at[e], sems.at[e, 2]),
        ]

    @pl.when(first)
    def _():
        for e in range(experts):
            for copy in copies(e):
                copy.start()

    slot_col = lax.broadcasted_iota(jnp.int32, (cap, 1), 0)
    slot_row = lax.broadcasted_iota(jnp.int32, (1, cap), 1)
    total = [None] * blocks
    for e in range(experts):
        chosen = []
        for b in range(blocks):
            at = slice(b * rows, (b + 1) * rows)
            pick = (rank_row_ref[e : e + 1, at] == slot_col).astype(jnp.bfloat16)
            chosen.append(
                jnp.dot(pick, x_ref[at, :], preferred_element_type=jnp.float32).astype(
                    jnp.bfloat16
                )
            )
        chosen = jnp.concatenate(chosen, axis=0)

        @pl.when(first)
        def _(e=e):
            for copy in copies(e):
                copy.wait()

        gate = jnp.dot(chosen, gate_ref[e], preferred_element_type=jnp.float32)
        up = jnp.dot(chosen, up_ref[e], preferred_element_type=jnp.float32)
        act = (gate / (1.0 + jnp.exp(-gate)) * up).astype(jnp.bfloat16)
        result = jnp.dot(act, down_ref[e], preferred_element_type=jnp.float32).astype(jnp.bfloat16)
        for b in range(blocks):
            at = slice(b * rows, (b + 1) * rows)
            place = (rank_ref[at, e : e + 1] == slot_row).astype(jnp.bfloat16)
            back = jnp.dot(
                place, result[b * cap : (b + 1) * cap, :], preferred_element_type=jnp.float32
            )
            back = back * weight_ref[at, e : e + 1]
            total[b] = back if e == 0 else total[b] + back
    for b in range(blocks):
        out_ref[b * rows : (b + 1) * rows, :] = total[b].astype(jnp.bfloat16)


def run_experts(x, rank, weight, w_gate, w_up, w_down, rows, cap):
    tokens, columns = x.shape
    experts, _, hidden = w_gate.shape
    blocks = 4
    span = blocks * rows
    extra = (-experts) % 8
    rank_row = jnp.pad(rank.T, ((0, extra), (0, 0)), constant_values=-1)
    any_spec = pl.BlockSpec(memory_space=pl.ANY)
    return pl.pallas_call(
        functools.partial(expert_kernel, experts, blocks, cap),
        grid=(tokens // span,),
        in_specs=[
            pl.BlockSpec((span, columns), lambda b: (b, 0)),
            pl.BlockSpec((span, experts), lambda b: (b, 0)),
            pl.BlockSpec((experts + extra, span), lambda b: (0, b)),
            pl.BlockSpec((span, experts), lambda b: (b, 0)),
            any_spec,
            any_spec,
            any_spec,
        ],
        out_specs=pl.BlockSpec((span, columns), lambda b: (b, 0)),
        out_shape=jax.ShapeDtypeStruct((tokens, columns), jnp.bfloat16),
        scratch_shapes=[
            pltpu.VMEM(w_gate.shape, jnp.bfloat16),
            pltpu.VMEM(w_up.shape, jnp.bfloat16),
            pltpu.VMEM(w_down.shape, jnp.bfloat16),
            pltpu.SemaphoreType.DMA((experts, 3)),
        ],
        compiler_params=pltpu.CompilerParams(vmem_limit_bytes=56 * 2**20),
        name="experts",
    )(x, rank, rank_row, weight, w_gate, w_up, w_down)


def local(
    resid_in,
    head_in,
    gate_in,
    in_basis,
    out_basis,
    step_size,
    decay_rate,
    init_state,
    lengths,
    norm_gain,
    out_proj,
    moe_gain,
    expert_ids,
    route_weight,
    placement,
    w_gate,
    w_up,
    w_down,
):
    tokens_total, lanes = head_in.shape
    model_width = out_proj.shape[1]
    devices = lax.axis_size("mix")
    me = lax.axis_index("mix")
    tok_rows = tokens_total // devices
    top_count = expert_ids.shape[1]
    experts_total = placement.shape[0]
    held = w_gate.shape[0]
    cap = 2 * tok_rows * top_count // experts_total

    slots = jnp.sum(
        jnp.where(
            expert_ids[:, :, None] == jnp.arange(experts_total, dtype=jnp.int32),
            placement,
            0,
        ),
        axis=2,
    )
    all_slots = lax.all_gather(slots, "mix", axis=0, tiled=True)
    all_weights = lax.all_gather(route_weight, "mix", axis=0, tiled=True)
    hits = all_slots[:, :, None] == me * held + jnp.arange(held, dtype=jnp.int32)
    named = jnp.any(hits, axis=1)
    weight = jnp.sum(jnp.where(hits, all_weights[:, :, None], 0.0), axis=1)
    below = jnp.tril(jnp.ones((tok_rows, tok_rows), jnp.bfloat16))
    count = jnp.einsum(
        "qt,bte->bqe",
        below,
        named.reshape(devices, tok_rows, held).astype(jnp.bfloat16),
        preferred_element_type=jnp.float32,
    )
    rank = jnp.where(named, count.reshape(tokens_total, held).astype(jnp.int32) - 1, -1)

    gain = lax.dynamic_slice(norm_gain, (me * lanes,), (lanes,)).reshape(1, lanes)
    mixed, squares = scan(
        head_in, gate_in, in_basis, out_basis, step_size, decay_rate, init_state, lengths, gain
    )
    squares = lax.psum_scatter(squares[0], "mix", scatter_dimension=0, tiled=True)
    mixer_sum = reduce_rows((mixed, out_proj), tok_rows, model_width, devices, 1)
    mixer_out = mixer_sum * lax.rsqrt(squares / (HEADS * HEAD_DIM) + epsilon)[:, None]
    hidden = resid_in.astype(jnp.float32) + mixer_out
    normed = (
        hidden * lax.rsqrt(jnp.mean(hidden * hidden, axis=1, keepdims=True) + epsilon) * moe_gain
    ).astype(jnp.bfloat16)
    everyone = gather_rows(normed, devices, 2)
    terms = run_experts(everyone, rank, weight, w_gate, w_up, w_down, tok_rows, cap)
    expert_sum = reduce_rows((terms,), tok_rows, model_width, devices, 3)
    return (hidden + expert_sum).astype(jnp.bfloat16)


def solution(mesh):
    return jax.shard_map(
        local,
        mesh=mesh,
        in_specs=(
            P(("groups", "mix"), None),
            P("groups", "mix"),
            P("groups", "mix"),
            P("groups", None),
            P("groups", None),
            P("mix", "groups"),
            P("mix"),
            P("groups", "mix", None, None),
            P("groups"),
            P(),
            P("mix", None),
            P(),
            P(("groups", "mix"), None),
            P(("groups", "mix"), None),
            P(),
            P("mix", None, None),
            P("mix", None, None),
            P("mix", None, None),
        ),
        out_specs=P(("groups", "mix"), None),
        check_vma=False,
    )
```

```python
import functools

import jax
import jax.numpy as jnp
from jax import lax
from jax.experimental import pallas as pl
from jax.experimental.pallas import tpu as pltpu
from jax.sharding import PartitionSpec as P

HEADS = 64
HEAD_DIM = 64
SPAN = 256
MESH = pl.DeviceIdType.MESH
NT = (((1,), (1,)), ((), ()))
TN = (((0,), (0,)), ((), ()))

epsilon = 1e-05


def scan_kernel(
    requests,
    heads,
    width,
    first_ref,
    x_ref,
    gate_ref,
    basis_ref,
    readout_ref,
    step_ref,
    decay_ref,
    init_ref,
    gain_ref,
    mixed_ref,
    square_ref,
    state_ref,
    source_ref,
):
    block = pl.program_id(0)
    rows = x_ref.shape[0]
    lanes = heads * width
    start = block * rows
    highest = lax.Precision.HIGHEST

    @pl.when(block == 0)
    def _():
        state_ref[...] = jnp.zeros_like(state_ref)

    pos_col = start + lax.broadcasted_iota(jnp.int32, (rows, 1), 0)
    pos_row = start + lax.broadcasted_iota(jnp.int32, (1, rows), 1)
    seg_col = jnp.zeros((rows, 1), jnp.int32)
    seg_row = jnp.zeros((1, rows), jnp.int32)
    seg_first = jnp.int32(0)
    seg_last = jnp.int32(0)
    for r in range(1, requests):
        first = first_ref[r]
        seg_col += (pos_col >= first).astype(jnp.int32)
        seg_row += (pos_row >= first).astype(jnp.int32)
        seg_first += (start >= first).astype(jnp.int32)
        seg_last += (start + rows - 1 >= first).astype(jnp.int32)
    carries = first_ref[seg_first] < start
    carries_last = first_ref[seg_last] < start
    same = (seg_col == seg_row) & (pos_row <= pos_col)
    total_col = lax.dot_general(
        same.astype(jnp.float32),
        decay_ref[...],
        NT,
        precision=highest,
        preferred_element_type=jnp.float32,
    )
    total_row = total_col.T
    step_row = step_ref[...]
    step_col = step_row.T
    readout = readout_ref[...]
    basis = basis_ref[...]
    scores = lax.dot_general(readout, basis, NT, preferred_element_type=jnp.float32)
    scores = jnp.where(same, scores, 0.0)

    def read(state):
        high = state.astype(jnp.bfloat16)
        low = (state - high.astype(jnp.float32)).astype(jnp.bfloat16)
        return lax.dot_general(
            readout, high, NT, preferred_element_type=jnp.float32
        ) + lax.dot_general(readout, low, NT, preferred_element_type=jnp.float32)

    carried = (seg_col == seg_first) & carries
    source_ref[...] = jnp.where(carried, read(state_ref[...]), 0.0)
    for r in range(requests):
        first = first_ref[r]

        @pl.when((first >= start) & (first < start + rows))
        def _(r=r):
            source_ref[...] += jnp.where(seg_col == r, read(init_ref[r]), 0.0)

    lane = lax.broadcasted_iota(jnp.int32, (1, lanes), 1)

    def spread(columns):
        out = columns[:, 0:1]
        for h in range(1, heads):
            out = jnp.where(lane >= h * width, columns[:, h : h + 1], out)
        return jnp.broadcast_to(out, (columns.shape[0], lanes))

    x = x_ref[...]
    parts = []
    for h in range(heads):
        gap = jnp.minimum(total_col[:, h : h + 1] - total_row[h : h + 1, :], 0.0)
        weight = jnp.exp(gap) * scores * step_row[h : h + 1, :]
        parts.append(
            jnp.dot(
                weight.astype(jnp.bfloat16),
                x[:, h * width : (h + 1) * width],
                preferred_element_type=jnp.float32,
            )
        )
    out = jnp.concatenate(parts, axis=1)
    out = out + spread(jnp.exp(total_col)) * source_ref[...]

    gate = gate_ref[...].astype(jnp.float32)
    gated = out * (gate / (1.0 + jnp.exp(-gate)))
    square_ref[...] = lax.dot_general(
        jnp.ones((8, lanes), jnp.float32),
        gated * gated,
        NT,
        precision=highest,
        preferred_element_type=jnp.float32,
    )
    mixed_ref[...] = (gated * gain_ref[...]).astype(jnp.bfloat16)

    last = total_col[rows - 1 : rows, :]
    keep = jnp.where(
        seg_col == seg_last, jnp.exp(jnp.minimum(last - total_col, 0.0)), 0.0
    )
    drive = (x.astype(jnp.float32) * spread(keep * step_col)).astype(jnp.bfloat16)
    added = lax.dot_general(drive, basis, TN, preferred_element_type=jnp.float32)
    fade = jnp.exp(last)
    for h in range(heads):
        at = slice(h * width, (h + 1) * width)
        source = jnp.where(carries_last, state_ref[at, :], init_ref[seg_last, at, :])
        state_ref[at, :] = added[at, :] + fade[:, h : h + 1] * source


def scan(head_in, gate_in, in_basis, out_basis, step_size, decay_rate, init_state, lengths, gain):
    tokens, lanes = head_in.shape
    heads = step_size.shape[0]
    width = lanes // heads
    requests = lengths.shape[0]
    states = in_basis.shape[1]
    rows = SPAN
    order = jnp.arange(requests, dtype=jnp.int32)
    first = jnp.sum(jnp.where(order[None, :] < order[:, None], lengths[None, :], 0), axis=1)
    extra = (-heads) % 8
    step = jnp.pad(step_size, ((0, extra), (0, 0)))
    decay = jnp.pad(-step_size * decay_rate[:, None], ((0, extra), (0, 0)))
    padded = heads + extra
    init = init_state.reshape(requests, lanes, states)
    return pl.pallas_call(
        functools.partial(scan_kernel, requests, heads, width),
        grid=(tokens // rows,),
        in_specs=[
            pl.BlockSpec(memory_space=pltpu.SMEM),
            pl.BlockSpec((rows, lanes), lambda b: (b, 0)),
            pl.BlockSpec((rows, lanes), lambda b: (b, 0)),
            pl.BlockSpec((rows, states), lambda b: (b, 0)),
            pl.BlockSpec((rows, states), lambda b: (b, 0)),
            pl.BlockSpec((padded, rows), lambda b: (0, b)),
            pl.BlockSpec((padded, rows), lambda b: (0, b)),
            pl.BlockSpec((requests, lanes, states), lambda b: (0, 0, 0)),
            pl.BlockSpec((1, lanes), lambda b: (0, 0)),
        ],
        out_specs=[
            pl.BlockSpec((rows, lanes), lambda b: (b, 0)),
            pl.BlockSpec((8, rows), lambda b: (0, b)),
        ],
        out_shape=[
            jax.ShapeDtypeStruct((tokens, lanes), jnp.bfloat16),
            jax.ShapeDtypeStruct((8, tokens), jnp.float32),
        ],
        scratch_shapes=[
            pltpu.VMEM((lanes, states), jnp.float32),
            pltpu.VMEM((rows, lanes), jnp.float32),
        ],
        compiler_params=pltpu.CompilerParams(vmem_limit_bytes=40 * 2**20),
        name="scan",
    )(first, head_in, gate_in, in_basis, out_basis, step, decay, init, gain)


def ring_of(ring):
    me = lax.axis_index("mix")
    core = me % 2
    pair = me // 2
    side = pair % 2
    along = pair // 2
    place = (1 - side) * along + side * (ring - 1 - along)
    return me, core, place, 1 - 2 * core


def device_at(place, core, ring):
    far = place // (ring // 2)
    along = (1 - far) * place + far * (ring - 1 - place)
    return (2 * along + far) * 2 + core


def greet(devices):
    barrier = pltpu.get_barrier_semaphore()
    for device in devices:
        pl.semaphore_signal(barrier, inc=1, device_id={"mix": device}, device_id_type=MESH)
    pl.semaphore_wait(barrier, len(devices))


def remote(src, dst, send, recv, device):
    return pltpu.make_async_remote_copy(
        src_ref=src,
        dst_ref=dst,
        send_sem=send,
        recv_sem=recv,
        device_id={"mix": device},
        device_id_type=MESH,
    )


def gather_kernel(ring, cuts, x_ref, out_ref, local_sem, ring_send, ring_recv, pair_send, pair_recv):
    me, core, place, way = ring_of(ring)
    rows = x_ref.shape[0]
    piece = rows // cuts
    onward = device_at((place + way + ring) % ring, core, ring)
    behind = device_at((place - way + ring) % ring, core, ring)
    twin = 2 * (me // 2) + 1 - core
    greet([onward, behind, twin])
    own = pltpu.make_async_copy(x_ref, out_ref.at[pl.ds(me * rows, rows), :], local_sem)
    own.start()
    ring_copies = {}
    pair_copies = {}
    for step in range(ring):
        holder = device_at((place - step * way + 2 * ring) % ring, core, ring)
        for c in range(cuts):
            at = out_ref.at[pl.ds(holder * rows + c * piece, piece), :]
            if step > 0:
                ring_copies[step - 1, c].wait_recv()
            src = x_ref.at[pl.ds(c * piece, piece), :] if step == 0 else at
            if step < ring - 1:
                copy = remote(src, at, ring_send.at[step, c], ring_recv.at[step, c], onward)
                copy.start()
                ring_copies[step, c] = copy
            copy = remote(src, at, pair_send.at[step, c], pair_recv.at[step, c], twin)
            copy.start()
            pair_copies[step, c] = copy
    own.wait()
    for copy in ring_copies.values():
        copy.wait_send()
    for copy in pair_copies.values():
        copy.wait_send()
        copy.wait_recv()


def gather_rows(x, devices, collective_id):
    rows, columns = x.shape
    ring = devices // 2
    cuts = 2
    return pl.pallas_call(
        functools.partial(gather_kernel, ring, cuts),
        in_specs=[pl.BlockSpec(memory_space=pltpu.VMEM)],
        out_specs=pl.BlockSpec(memory_space=pl.ANY),
        out_shape=jax.ShapeDtypeStruct((devices * rows, columns), x.dtype),
        scratch_shapes=[
            pltpu.SemaphoreType.DMA,
            pltpu.SemaphoreType.DMA((ring, cuts)),
            pltpu.SemaphoreType.DMA((ring, cuts)),
            pltpu.SemaphoreType.DMA((ring, cuts)),
            pltpu.SemaphoreType.DMA((ring, cuts)),
        ],
        compiler_params=pltpu.CompilerParams(
            collective_id=collective_id, has_side_effects=True, vmem_limit_bytes=48 * 2**20
        ),
        name="gather_rows",
    )(x)


def reduce_kernel(
    ring,
    cuts,
    product,
    *refs,
):
    if product:
        mixed_ref, proj_ref, side_ref, out_ref, sides_ref = refs[:5]
        refs = refs[5:]
        side_rows = side_ref.shape[0]
        local_sem, side_send, side_recv, side_pair_send, side_pair_recv = refs[-5:]
        to_twin, mine, from_twin, sent, got = refs[:5]
        refs = refs[5:]
    else:
        terms_ref, out_ref = refs[:2]
        refs = refs[2:]
        mine, from_twin, sent, got = refs[:4]
        mine_sem = refs[-1]
        refs = refs[4:]
    pair_send, pair_recv, ring_send, ring_recv = refs[:4]
    me, core, place, way = ring_of(ring)
    rows = out_ref.shape[0]
    piece = rows // cuts
    onward = device_at((place + way + ring) % ring, core, ring)
    behind = device_at((place - way + ring) % ring, core, ring)
    twin = 2 * (me // 2) + 1 - core
    greet([onward, behind, twin])
    pair_copies = []
    mine_copies = []
    side_copies = {}
    side_pairs = []

    def pass_side(step):
        holder = device_at((place - step * way + 2 * ring) % ring, core, ring)
        at = sides_ref.at[pl.ds(holder * side_rows, side_rows), :]
        if step > 0:
            side_copies[step - 1].wait_recv()
        src = side_ref if step == 0 else at
        if step < ring - 1:
            copy = remote(src, at, side_send.at[step], side_recv.at[step], onward)
            copy.start()
            side_copies[step] = copy
        copy = remote(src, at, side_pair_send.at[step], side_pair_recv.at[step], twin)
        copy.start()
        side_pairs.append(copy)

    if product:
        own = pltpu.make_async_copy(
            side_ref, sides_ref.at[pl.ds(me * side_rows, side_rows), :], local_sem
        )
        own.start()

    def give(step):
        theirs = device_at((place + (1 + step) * way) % ring, 1 - core, ring)
        if product:
            to_twin[step] = jnp.dot(
                mixed_ref[pl.ds(theirs * rows, rows), :],
                proj_ref[...],
                preferred_element_type=jnp.float32,
            ).astype(jnp.bfloat16)
            src = to_twin.at[step]
        else:
            src = terms_ref.at[pl.ds(theirs * rows, rows), :]
        copy = remote(src, from_twin.at[step], pair_send.at[step], pair_recv.at[step], twin)
        copy.start()
        pair_copies.append(copy)
        ours = device_at((place - (1 + step) * way + 2 * ring) % ring, core, ring)
        if product:
            mine[step] = jnp.dot(
                mixed_ref[pl.ds(ours * rows, rows), :],
                proj_ref[...],
                preferred_element_type=jnp.float32,
            ).astype(jnp.bfloat16)
        else:
            copy = pltpu.make_async_copy(
                terms_ref.at[pl.ds(ours * rows, rows), :], mine.at[step], mine_sem.at[step]
            )
            copy.start()
            mine_copies.append(copy)

    if product:
        give(0)
        pass_side(0)
    else:
        for step in range(ring):
            give(step)
    ring_copies = {}
    for step in range(ring):
        if product and step + 1 < ring:
            give(step + 1)
            pass_side(step + 1)
        if not product:
            mine_copies[step].wait()
        pair_copies[step].wait_recv()
        for c in range(cuts):
            at = pl.ds(c * piece, piece)
            total = mine[step, at, :].astype(jnp.float32) + from_twin[step, at, :].astype(
                jnp.float32
            )
            if step > 0:
                ring_copies[step - 1, c].wait_recv()
                total = total + got[step - 1, at, :].astype(jnp.float32)
            if step < ring - 1:
                sent[step, at, :] = total.astype(jnp.bfloat16)
                copy = remote(
                    sent.at[step, at, :],
                    got.at[step, at, :],
                    ring_send.at[step, c],
                    ring_recv.at[step, c],
                    onward,
                )
                copy.start()
                ring_copies[step, c] = copy
            else:
                out_ref[at, :] = total
    for copy in pair_copies:
        copy.wait_send()
    for copy in ring_copies.values():
        copy.wait_send()
    if product:
        own.wait()
        for copy in side_copies.values():
            copy.wait_send()
        for copy in side_pairs:
            copy.wait_send()
            copy.wait_recv()


def reduce_rows(operands, rows, columns, devices, collective_id):
    product = len(operands) == 3
    ring = devices // 2
    cuts = 2
    block = pltpu.VMEM((ring, rows, columns), jnp.bfloat16)
    short = pltpu.VMEM((ring - 1, rows, columns), jnp.bfloat16)
    return pl.pallas_call(
        functools.partial(reduce_kernel, ring, cuts, product),
        in_specs=[pl.BlockSpec(memory_space=pltpu.VMEM if product else pl.ANY)] * len(operands),
        out_specs=[pl.BlockSpec(memory_space=pltpu.VMEM)] * (2 if product else 1),
        out_shape=[jax.ShapeDtypeStruct((rows, columns), jnp.float32)]
        + (
            [jax.ShapeDtypeStruct((devices * operands[2].shape[0], rows), jnp.float32)]
            if product
            else []
        ),
        scratch_shapes=([block] if product else [])
        + [block, block, short, short]
        + [
            pltpu.SemaphoreType.DMA((ring,)),
            pltpu.SemaphoreType.DMA((ring,)),
            pltpu.SemaphoreType.DMA((ring, cuts)),
            pltpu.SemaphoreType.DMA((ring, cuts)),
        ]
        + (
            [pltpu.SemaphoreType.DMA] + [pltpu.SemaphoreType.DMA((ring,))] * 4
            if product
            else [pltpu.SemaphoreType.DMA((ring,))]
        ),
        compiler_params=pltpu.CompilerParams(
            collective_id=collective_id, has_side_effects=True, vmem_limit_bytes=52 * 2**20
        ),
        name="reduce_products" if product else "reduce_rows",
    )(*operands)


def expert_kernel(
    experts, blocks, cap, x_ref, rank_ref, rank_row_ref, weight_ref, gate_hbm, up_hbm, down_hbm,
    out_ref, gate_ref, up_ref, down_ref, sems,
):
    first = pl.program_id(0) == 0
    rows = x_ref.shape[0] // blocks

    def copies(e):
        return [
            pltpu.make_async_copy(gate_hbm.at[e], gate_ref.at[e], sems.at[e, 0]),
            pltpu.make_async_copy(up_hbm.at[e], up_ref.at[e], sems.at[e, 1]),
            pltpu.make_async_copy(down_hbm.at[e], down_ref.at[e], sems.at[e, 2]),
        ]

    @pl.when(first)
    def _():
        for e in range(experts):
            for copy in copies(e):
                copy.start()

    slot_col = lax.broadcasted_iota(jnp.int32, (cap, 1), 0)
    slot_row = lax.broadcasted_iota(jnp.int32, (1, cap), 1)
    total = [None] * blocks
    for e in range(experts):
        chosen = []
        for b in range(blocks):
            at = slice(b * rows, (b + 1) * rows)
            pick = (rank_row_ref[e : e + 1, at] == slot_col).astype(jnp.bfloat16)
            chosen.append(
                jnp.dot(pick, x_ref[at, :], preferred_element_type=jnp.float32).astype(
                    jnp.bfloat16
                )
            )
        chosen = jnp.concatenate(chosen, axis=0)

        @pl.when(first)
        def _(e=e):
            for copy in copies(e):
                copy.wait()

        gate = jnp.dot(chosen, gate_ref[e], preferred_element_type=jnp.float32)
        up = jnp.dot(chosen, up_ref[e], preferred_element_type=jnp.float32)
        act = (gate / (1.0 + jnp.exp(-gate)) * up).astype(jnp.bfloat16)
        result = jnp.dot(act, down_ref[e], preferred_element_type=jnp.float32).astype(jnp.bfloat16)
        for b in range(blocks):
            at = slice(b * rows, (b + 1) * rows)
            place = (rank_ref[at, e : e + 1] == slot_row).astype(jnp.bfloat16)
            back = jnp.dot(
                place, result[b * cap : (b + 1) * cap, :], preferred_element_type=jnp.float32
            )
            back = back * weight_ref[at, e : e + 1]
            total[b] = back if e == 0 else total[b] + back
    for b in range(blocks):
        out_ref[b * rows : (b + 1) * rows, :] = total[b].astype(jnp.bfloat16)


def run_experts(x, rank, weight, w_gate, w_up, w_down, rows, cap):
    tokens, columns = x.shape
    experts, _, hidden = w_gate.shape
    blocks = 4
    span = blocks * rows
    extra = (-experts) % 8
    rank_row = jnp.pad(rank.T, ((0, extra), (0, 0)), constant_values=-1)
    any_spec = pl.BlockSpec(memory_space=pl.ANY)
    return pl.pallas_call(
        functools.partial(expert_kernel, experts, blocks, cap),
        grid=(tokens // span,),
        in_specs=[
            pl.BlockSpec((span, columns), lambda b: (b, 0)),
            pl.BlockSpec((span, experts), lambda b: (b, 0)),
            pl.BlockSpec((experts + extra, span), lambda b: (0, b)),
            pl.BlockSpec((span, experts), lambda b: (b, 0)),
            any_spec,
            any_spec,
            any_spec,
        ],
        out_specs=pl.BlockSpec((span, columns), lambda b: (b, 0)),
        out_shape=jax.ShapeDtypeStruct((tokens, columns), jnp.bfloat16),
        scratch_shapes=[
            pltpu.VMEM(w_gate.shape, jnp.bfloat16),
            pltpu.VMEM(w_up.shape, jnp.bfloat16),
            pltpu.VMEM(w_down.shape, jnp.bfloat16),
            pltpu.SemaphoreType.DMA((experts, 3)),
        ],
        compiler_params=pltpu.CompilerParams(vmem_limit_bytes=56 * 2**20),
        name="experts",
    )(x, rank, rank_row, weight, w_gate, w_up, w_down)


def local(
    resid_in,
    head_in,
    gate_in,
    in_basis,
    out_basis,
    step_size,
    decay_rate,
    init_state,
    lengths,
    norm_gain,
    out_proj,
    moe_gain,
    expert_ids,
    route_weight,
    placement,
    w_gate,
    w_up,
    w_down,
):
    tokens_total, lanes = head_in.shape
    model_width = out_proj.shape[1]
    devices = lax.axis_size("mix")
    me = lax.axis_index("mix")
    tok_rows = tokens_total // devices
    top_count = expert_ids.shape[1]
    experts_total = placement.shape[0]
    held = w_gate.shape[0]
    cap = 2 * tok_rows * top_count // experts_total

    slots = jnp.sum(
        jnp.where(
            expert_ids[:, :, None] == jnp.arange(experts_total, dtype=jnp.int32),
            placement,
            0,
        ),
        axis=2,
    )
    gain = lax.dynamic_slice(norm_gain, (me * lanes,), (lanes,)).reshape(1, lanes)
    mixed, squares = scan(
        head_in, gate_in, in_basis, out_basis, step_size, decay_rate, init_state, lengths, gain
    )
    side = jnp.concatenate(
        [slots.T.astype(jnp.float32), route_weight.T, squares[0].reshape(devices, tok_rows)], axis=0
    )
    mixer_sum, sides = reduce_rows((mixed, out_proj, side), tok_rows, model_width, devices, 1)
    sides = sides.reshape(devices, 2 * top_count + devices, tok_rows)
    squares = jnp.sum(
        lax.dynamic_index_in_dim(sides, 2 * top_count + me, axis=1, keepdims=False), axis=0
    )
    all_slots = sides[:, :top_count, :, None].astype(jnp.int32)
    hits = all_slots == me * held + jnp.arange(held, dtype=jnp.int32)
    named = jnp.any(hits, axis=1)
    weight = jnp.sum(jnp.where(hits, sides[:, top_count : 2 * top_count, :, None], 0.0), axis=1)
    weight = weight.reshape(tokens_total, held)
    below = jnp.tril(jnp.ones((tok_rows, tok_rows), jnp.bfloat16))
    count = jnp.einsum(
        "qt,bte->bqe", below, named.astype(jnp.bfloat16), preferred_element_type=jnp.float32
    )
    rank = jnp.where(named, count.astype(jnp.int32) - 1, -1).reshape(tokens_total, held)
    mixer_out = mixer_sum * lax.rsqrt(squares / (HEADS * HEAD_DIM) + epsilon)[:, None]
    hidden = resid_in.astype(jnp.float32) + mixer_out
    normed = (
        hidden * lax.rsqrt(jnp.mean(hidden * hidden, axis=1, keepdims=True) + epsilon) * moe_gain
    ).astype(jnp.bfloat16)
    everyone = gather_rows(normed, devices, 2)
    terms = run_experts(everyone, rank, weight, w_gate, w_up, w_down, tok_rows, cap)
    (expert_sum,) = reduce_rows((terms,), tok_rows, model_width, devices, 3)
    return (hidden + expert_sum).astype(jnp.bfloat16)


def solution(mesh):
    return jax.shard_map(
        local,
        mesh=mesh,
        in_specs=(
            P(("groups", "mix"), None),
            P("groups", "mix"),
            P("groups", "mix"),
            P("groups", None),
            P("groups", None),
            P("mix", "groups"),
            P("mix"),
            P("groups", "mix", None, None),
            P("groups"),
            P(),
            P("mix", None),
            P(),
            P(("groups", "mix"), None),
            P(("groups", "mix"), None),
            P(),
            P("mix", None, None),
            P("mix", None, None),
            P("mix", None, None),
        ),
        out_specs=P(("groups", "mix"), None),
        check_vma=False,
    )
```
